32 devices in a mesh: pair: 4 (over y, x), feat: 8 (over z, core).
Axes of the slice: x: 2, y: 2, z: 4, core: 2. Of those that a mesh axis runs over, the one named last changes fastest.
Arguments:
- decoder: float32 [8, 16384, 2048], P('pair', 'feat'), may hold values from -0.3125 to 0.3125
- pair_map: int32 [8, 2], P('pair'), may hold values from 0 to 3, as said below
- indices: int32 [3, 256, 128], replicated, may hold values from 0 to 16383, as said below
- values: float32 [3, 256, 128], replicated, may hold values from 0.2 to 3
- target: float32 [3, 256, 2048], P(None, ('pair', 'feat')), may hold values from -6 to 6
Outputs:
- recon: bfloat16 [3, 256, 2048], P(None, ('pair', 'feat'))
- dec_grad: float32 [8, 16384, 2048], P('pair', 'feat')
- feat_grad: float32 [3, 256, 128], P(None, ('pair', 'feat'))
The draws below stay inside these ranges and needn't reach their ends.
Inputs may be any that keep to these rules, and one draw needn't show every extreme that they name: `pair_map`: each pair (s, t) of layers with s <= t < 3 stands in exactly one row as (s, t); every other row is (3, 3), an empty slot. For each layer and token the 128 indices are distinct.
All inputs are finite; a program needn't handle non-finite values.
Results may differ from the reference program's by a relative error of at most 0.0027.
Values may be sent and summed in bfloat16 or wider, within the bound.
No kernel may reach another device: no remote copies, remote signals or barrier semaphores. Data moves between devices by JAX's collectives and lax.ppermute only.
A program may use at most 192 MiB of HBM per device.

```python
import math
import jax
import jax.numpy as jnp
import numpy as np
from jax import lax

D = 2048
F = 16384
L = 3
K = 128
TOK = 256
SLOTS = 8


def draw_indices(key, part):
    scores = jax.random.randint(key, (L, TOK, F), 0, 2 ** 30)
    ranked = jnp.argsort(scores, axis=-1, stable=True)
    return ranked[:, :, :K].astype(jnp.int32)


def draw_pair_map(key, part):
    listing = [(source, target_layer) for target_layer in range(L) for source in range(target_layer + 1)]
    listing = listing + [(L, L)] * (SLOTS - len(listing))
    table = jnp.asarray(np.array(listing, dtype=np.int32))
    shuffled = jax.random.permutation(jax.random.fold_in(key, 7), SLOTS)
    return table[shuffled].astype(jnp.int32)


def level_of(rng, dims, cuts, least, largest):
    loudness = 1.0
    for axis_at, blocks in cuts:
        heights = jax.random.uniform(jax.random.fold_in(jax.random.fold_in(rng, 6), axis_at), (blocks,), jnp.float32, least / len(cuts), largest / len(cuts))
        loudness = loudness * jnp.repeat(jnp.exp(heights), dims[axis_at] // blocks).reshape((-1,) + (1,) * (len(dims) - 1 - axis_at))
    return loudness


def gaussian(rng, extent, width, limit, split=(), kind=jnp.bfloat16):
    level = level_of(rng, extent, split, -0.22, 0.18) if split else 1.0
    values = jax.random.normal(rng, extent, jnp.float32) * width * level
    return jnp.minimum(jnp.maximum(values, -limit), limit).astype(kind)


def setup_inputs(seed: int = 0) -> dict:
    key_of = jax.random.split(jax.random.key(seed), 6)
    decoder = gaussian(key_of[0], (SLOTS, F, D), (K * L) ** -0.5, 0.3125, ((0, 4), (1, 8)), jnp.float32)
    pair_map = draw_pair_map(jax.random.fold_in(key_of[5], 71), 0)
    indices = draw_indices(jax.random.fold_in(key_of[5], 71), 0)
    values = jnp.clip(jnp.exp(jax.random.uniform(key_of[3], (L, TOK, K), jnp.float32, math.log(0.2), math.log(3.0))), 0.2, 3.0)
    target = gaussian(key_of[4], (L, TOK, D), 1.0, 6.0, ((1, 32),), jnp.float32)
    return dict(decoder=decoder, pair_map=pair_map, indices=indices, values=values, target=target)


def reference(decoder, pair_map, indices, values, target):
    layer_axis = jnp.arange(L, dtype=jnp.int32)[:, None, None]
    token_axis = jnp.arange(TOK, dtype=jnp.int32)[None, :, None]
    dense_acts = jnp.zeros((L, TOK, F), jnp.float32).at[layer_axis, token_axis, indices].set(values)
    sources = pair_map[:, 0]
    targets = pair_map[:, 1]

    def recon_step(running, slot_data):
        decoder_tile, source, target_layer = slot_data
        picked = jnp.minimum(source, L - 1)
        product = jnp.dot(dense_acts[picked], decoder_tile, precision=lax.Precision.HIGHEST, preferred_element_type=jnp.float32)
        choose = jax.nn.one_hot(target_layer, L, dtype=jnp.float32)
        return running + choose[:, None, None] * product[None], None

    full, _ = lax.scan(recon_step, jnp.zeros((L, TOK, D), jnp.float32), (decoder, sources, targets))
    recon = full.astype(jnp.bfloat16)
    error = (full - target).astype(jnp.bfloat16)
    error_wide = error.astype(jnp.float32)

    def grad_step(grad_dense, slot_data):
        decoder_tile, source, target_layer = slot_data
        is_live = (target_layer < L).astype(jnp.float32)
        picked = jnp.minimum(source, L - 1)
        slot_error = error_wide[jnp.minimum(target_layer, L - 1)] * is_live
        tile_grad = jnp.dot(dense_acts[picked].T, slot_error, precision=lax.Precision.HIGHEST, preferred_element_type=jnp.float32)
        back = jnp.dot(slot_error, decoder_tile.T, precision=lax.Precision.HIGHEST, preferred_element_type=jnp.float32)
        choose = jax.nn.one_hot(source, L, dtype=jnp.float32)
        return grad_dense + choose[:, None, None] * back[None], tile_grad

    grad_dense, dec_grad = lax.scan(grad_step, jnp.zeros((L, TOK, F), jnp.float32), (decoder, sources, targets))
    feat_grad = jnp.take_along_axis(grad_dense, indices, axis=2)
    return recon, dec_grad, feat_grad
```

```python
import jax
import jax.numpy as jnp
from jax import lax
from jax.experimental import pallas as pl
from jax.experimental.pallas import tpu as pltpu
from jax.sharding import PartitionSpec as P

f32=jnp.float32
bf16=jnp.bfloat16
WIRE_SCALE=128.0
LANES=128
NT=(((1,),(1,)),((),()))
TN=(((0,),(0,)),((),()))

def split(x):
    hi=x.astype(bf16)
    return hi,(x-hi.astype(f32)).astype(bf16)

def build_acts(first, idx_ref, val_ref, hi_out, lo_out, rows_scr, code_scr):
    T=idx_ref.shape[1]; K=idx_ref.shape[2]; W=hi_out.shape[-1]; H=W//LANES
    TB=rows_scr.shape[0]//(2*H)
    iota_h=lax.broadcasted_iota(jnp.int32,(H,K),0)
    iota_l=lax.broadcasted_iota(jnp.int32,(LANES,K),0)
    def block(b,_):
        base=pl.multiple_of(b*TB,TB)
        def eight(g,_):
            r0=pl.multiple_of(base+g*8,8)
            for i in range(8):
                ids=idx_ref[0,pl.ds(r0+i,1),:]-first
                v=val_ref[0,pl.ds(r0+i,1),:]
                vh,vl=split(v)
                hi=ids>>7
                lo=ids&127
                hit=hi==iota_h
                a=jnp.concatenate([jnp.where(hit,vh.astype(f32),0.0),jnp.where(hit,vl.astype(f32),0.0)],axis=0).astype(bf16)
                oh=jnp.where(lo==iota_l,1.0,0.0).astype(bf16)
                r=lax.dot_general(a,oh,NT,preferred_element_type=f32)
                rows_scr[pl.ds(pl.multiple_of((g*8+i)*2*H,2*H),2*H),:]=r
            return 0
        lax.fori_loop(0,TB//8,eight,0)
        for h in range(H):
            hi_out[pl.ds(base,TB),h*LANES:(h+1)*LANES]=rows_scr[pl.ds(h,TB,stride=2*H),:].astype(bf16)
            lo_out[pl.ds(base,TB),h*LANES:(h+1)*LANES]=rows_scr[pl.ds(H+h,TB,stride=2*H),:].astype(bf16)
        return 0
    lax.fori_loop(0,T//TB,block,0)

def build_kernel(src_ref, first_ref, idx_ref, val_ref, hi_ref, lo_ref, rows_scr):
    build_acts(first_ref[0], idx_ref, val_ref, hi_ref.at[0], lo_ref.at[0], rows_scr, None)

def build_call(src, first, indices, values, W, TB=64):
    S=src.shape[0]; L,T,K=indices.shape; H=W//LANES
    return pl.pallas_call(build_kernel,
        out_shape=(jax.ShapeDtypeStruct((S,T,W),bf16),)*2,
        grid_spec=pltpu.PrefetchScalarGridSpec(num_scalar_prefetch=2, grid=(S,),
            in_specs=[pl.BlockSpec((1,T,K),lambda j,s,f:(s[j],0,0))]*2,
            out_specs=[pl.BlockSpec((1,T,W),lambda j,s,f:(j,0,0))]*2,
            scratch_shapes=[pltpu.VMEM((TB*2*H,LANES),f32)]),
        compiler_params=pltpu.CompilerParams(vmem_limit_bytes=40<<20),
        name="build")(src,first,indices,values)

def recon_kernel(src_ref, first_ref, idx_ref, val_ref, dec_ref, prod_ref, hi_ref, lo_ref, rows_scr):
    @pl.when(pl.program_id(1)==0)
    def _(): build_acts(first_ref[0], idx_ref, val_ref, hi_ref.at[0], lo_ref.at[0], rows_scr, None)
    dh,dl=split(dec_ref[0])
    ah=hi_ref[0]
    p=jnp.dot(ah,dh,preferred_element_type=f32)
    p+=jnp.dot(lo_ref[0],dh,preferred_element_type=f32)
    p+=jnp.dot(ah,dl,preferred_element_type=f32)
    prod_ref[0]=p

def recon_call(src, first, indices, values, dec, TB=64, DT=512, nbuf=3):
    S,W,D=dec.shape; L,T,K=indices.shape; H=W//LANES
    return pl.pallas_call(recon_kernel,
        out_shape=(jax.ShapeDtypeStruct((S,T,D),f32),jax.ShapeDtypeStruct((S,T,W),bf16),jax.ShapeDtypeStruct((S,T,W),bf16)),
        grid_spec=pltpu.PrefetchScalarGridSpec(num_scalar_prefetch=2, grid=(S,D//DT),
            in_specs=[pl.BlockSpec((1,T,K),lambda j,n,s,f:(s[j],0,0))]*2+[pl.BlockSpec((1,W,DT),lambda j,n,s,f:(j,0,n))],
            out_specs=[pl.BlockSpec((1,T,DT),lambda j,n,s,f:(j,0,n))]+[pl.BlockSpec((1,T,W),lambda j,n,s,f:(j,0,0))]*2,
            scratch_shapes=[pltpu.VMEM((TB*2*H,LANES),f32)]),
        compiler_params=pltpu.CompilerParams(vmem_limit_bytes=56<<20),
        name="recon")(src,first,indices,values,dec)

def back_kernel(src_ref, first_ref, idx_ref, err_ref, dec_ref, out_ref):
    n=pl.program_id(1)
    FT=dec_ref.shape[1]
    @pl.when(n==0)
    def _(): out_ref[...]=jnp.zeros_like(out_ref)
    dh,dl=split(dec_ref[0])
    e=err_ref[0]
    g=lax.dot_general(e,dh,NT,preferred_element_type=f32)
    g+=lax.dot_general(e,dl,NT,preferred_element_type=f32)
    ids=idx_ref[0]-(first_ref[0]+n*FT)
    hi=ids>>7
    lo=ids&127
    acc=out_ref[0]
    for c in range(FT//LANES):
        acc=jnp.where(hi==c,jnp.take_along_axis(g[:,c*LANES:(c+1)*LANES],lo,axis=1),acc)
    out_ref[0]=acc

def back_call(src, first, indices, err, dec, FT=512, nbuf=2):
    S,W,D=dec.shape; L,T,K=indices.shape
    FT=min(FT,W)
    return pl.pallas_call(back_kernel,
        out_shape=jax.ShapeDtypeStruct((S,T,K),f32),
        grid_spec=pltpu.PrefetchScalarGridSpec(num_scalar_prefetch=2, grid=(S,W//FT),
            in_specs=[pl.BlockSpec((1,T,K),lambda j,n,s,f:(s[j],0,0)),pl.BlockSpec((1,T,D),lambda j,n,s,f:(j,0,0)),
                      pl.BlockSpec((1,FT,D),lambda j,n,s,f:(j,n,0))],
            out_specs=pl.BlockSpec((1,T,K),lambda j,n,s,f:(j,0,0))),
        compiler_params=pltpu.CompilerParams(vmem_limit_bytes=56<<20),
        name="back")(src,first,indices,err,dec)

def grad_kernel(hi_ref, lo_ref, err_ref, out_ref):
    e=err_ref[0]
    p=lax.dot_general(hi_ref[0],e,TN,preferred_element_type=f32)
    out_ref[0]=p+lax.dot_general(lo_ref[0],e,TN,preferred_element_type=f32)

def grad_call(hi, lo, err, FT=512):
    S,T,W=hi.shape; D=err.shape[2]
    FT=min(FT,W)
    return pl.pallas_call(grad_kernel,
        out_shape=jax.ShapeDtypeStruct((S,W,D),f32),
        grid=(S,W//FT),
        in_specs=[pl.BlockSpec((1,T,FT),lambda j,n:(j,0,n))]*2+[pl.BlockSpec((1,T,D),lambda j,n:(j,0,0))],
        out_specs=pl.BlockSpec((1,FT,D),lambda j,n:(j,n,0)),
        compiler_params=pltpu.CompilerParams(vmem_limit_bytes=56<<20),
        name="grad")(hi,lo,err)


def parts_of(feat_count):
    return feat_count // 2


def swap_cores(x):
    count = lax.axis_size("feat")
    return lax.ppermute(x, "feat", [(i, i ^ 1) for i in range(count)])


def shift_z(x, step):
    count = lax.axis_size("feat")
    return lax.ppermute(x, "feat", [(i, (i + 2 * step) % count) for i in range(count)])


def shift_pair(x, step):
    count = lax.axis_size("pair")
    return lax.ppermute(x, "pair", [(i, (i + step) % count) for i in range(count)])


def take(x, at, axis):
    return lax.dynamic_index_in_dim(x, at, axis, keepdims=False)


def pack(x):
    return (x * WIRE_SCALE).astype(jnp.float16)


def unpack(x):
    return x.astype(f32) * (1.0 / WIRE_SCALE)


def sum_full(prod, goals_all, layers):
    pairs, zs = lax.axis_size("pair"), lax.axis_size("feat") // 2
    p, feat = lax.axis_index("pair"), lax.axis_index("feat")
    z, core = feat // 2, feat % 2
    slots, tokens, width = prod.shape
    rows = tokens // (pairs * zs * 2)
    cut = prod.reshape(slots, pairs, zs, 2, rows, width)
    got = swap_cores(pack(take(cut, 1 - core, 3)))
    half = take(cut, core, 3) + unpack(got)
    arrived = [(p, take(half, p, 1))]
    for step in range(1, pairs):
        sent = pack(take(half, (p + step) % pairs, 1))
        arrived.append(((p - step) % pairs, unpack(shift_pair(sent, step))))
    layer_list = []
    for layer in range(layers):
        total = jnp.zeros(half.shape[2:], f32)
        for owner, block in arrived:
            goals = take(goals_all, owner, 0)
            for j in range(slots):
                total = total + jnp.where(goals[j] == layer, block[j], 0.0)
        layer_list.append(total)
    summed = jnp.stack(layer_list)
    full = take(summed, z, 1)
    for step in range(1, zs):
        full = full + unpack(shift_z(pack(take(summed, (z + step) % zs, 1)), step))
    return full


def spread_errors(error, goals_all):
    pairs, zs = lax.axis_size("pair"), lax.axis_size("feat") // 2
    p, feat = lax.axis_index("pair"), lax.axis_index("feat")
    z, core = feat // 2, feat % 2
    layers, rows, width = error.shape
    slots = goals_all.shape[1]
    column = jnp.zeros((layers, zs, rows, width), bf16)
    column = lax.dynamic_update_index_in_dim(column, error, z, 1)
    for step in range(1, zs):
        column = lax.dynamic_update_index_in_dim(column, shift_z(error, step), (z - step) % zs, 1)

    def choose(owner):
        goals = take(goals_all, owner, 0)
        return jnp.stack([
            jnp.where(goals[j] < layers, take(column, jnp.minimum(goals[j], layers - 1), 0), jnp.zeros((), bf16))
            for j in range(slots)
        ])

    plane = jnp.zeros((slots, pairs, zs, rows, width), bf16)
    plane = lax.dynamic_update_index_in_dim(plane, choose(p), p, 1)
    for step in range(1, pairs):
        got = shift_pair(choose((p + step) % pairs), step)
        plane = lax.dynamic_update_index_in_dim(plane, got, (p - step) % pairs, 1)
    other = swap_cores(plane)
    both = jnp.stack([jnp.where(core == 0, plane, other), jnp.where(core == 0, other, plane)], axis=3)
    return both.reshape(slots, pairs * zs * 2 * rows, width)


def sum_picks(picks, sources_all, layers):
    pairs, zs = lax.axis_size("pair"), lax.axis_size("feat") // 2
    p, feat = lax.axis_index("pair"), lax.axis_index("feat")
    z, core = feat // 2, feat % 2
    slots, tokens, width = picks.shape
    rows = tokens // (pairs * zs * 2)
    cut = picks.reshape(slots, pairs, zs, 2, rows, width)
    half = take(cut, core, 3) + swap_cores(take(cut, 1 - core, 3))
    column = take(half, z, 2)
    for step in range(1, zs):
        column = column + shift_z(take(half, (z + step) % zs, 2), step)
    arrived = [(p, take(column, p, 1))]
    for step in range(1, pairs):
        sent = take(column, (p + step) % pairs, 1)
        arrived.append(((p - step) % pairs, shift_pair(sent, step)))
    layer_list = []
    for layer in range(layers):
        total = jnp.zeros((rows, width), f32)
        for owner, block in arrived:
            sources = take(sources_all, owner, 0)
            for j in range(slots):
                total = total + jnp.where(sources[j] == layer, block[j], 0.0)
        layer_list.append(total)
    return jnp.stack(layer_list)


def body(decoder, pair_map, indices, values, target):
    slots, block_width, width = decoder.shape
    layers, tokens, active = indices.shape
    pairs = lax.axis_size("pair")
    first = (lax.axis_index("feat") * block_width).reshape(1).astype(jnp.int32)
    source = jnp.minimum(pair_map[:, 0], layers - 1)
    pair_all = lax.all_gather(pair_map, "pair", axis=0)
    sources_all, goals_all = pair_all[:, :, 0], pair_all[:, :, 1]
    prod, hi, lo = recon_call(source, first, indices, values, decoder)
    full = sum_full(prod, goals_all, layers)
    recon = full.astype(bf16)
    error = (full - target).astype(bf16)
    slot_error = spread_errors(error, goals_all)
    picks = back_call(source, first, indices, slot_error, decoder)
    feat_grad = sum_picks(picks, sources_all, layers)
    dec_grad = grad_call(hi, lo, slot_error)
    return recon, dec_grad, feat_grad


def solution(mesh):
    in_specs = (P("pair", "feat", None), P("pair", None), P(), P(), P(None, ("pair", "feat"), None))
    out_specs = (
        P(None, ("pair", "feat"), None),
        P("pair", "feat", None),
        P(None, ("pair", "feat"), None),
    )
    return jax.shard_map(body, mesh=mesh, in_specs=in_specs, out_specs=out_specs, check_vma=False)
```

```python
import jax
import jax.numpy as jnp
from jax import lax
from jax.experimental import pallas as pl
from jax.experimental.pallas import tpu as pltpu
from jax.sharding import PartitionSpec as P

f32 = jnp.float32
bf16 = jnp.bfloat16
i32 = jnp.int32
LANES = 128
WIRE_SCALE = 128.0
VMEM_LIMIT = 56 << 20
NT = (((1,), (1,)), ((), ()))
TN = (((0,), (0,)), ((), ()))


def split(x):
    hi = x.astype(bf16)
    return hi, (x - hi.astype(f32)).astype(bf16)


def cost(flops, nbytes):
    return pl.CostEstimate(flops=int(flops), bytes_accessed=int(nbytes), transcendentals=0)


def params():
    return pltpu.CompilerParams(vmem_limit_bytes=VMEM_LIMIT)


def lay_out(features, idx_ref, val_ref, ids_ref, val_scr, pairs, zs):
    tokens = idx_ref.shape[1]
    rows = tokens // (pairs * zs * 2)
    p, feat = lax.axis_index("pair"), lax.axis_index("feat")
    first = feat * features

    def run(at, _):
        zr = at & (zs - 1)
        pr = (at // zs) & (pairs - 1)
        cr = at // (zs * pairs)
        block = (p ^ pr) * (zs * 2) + (feat ^ (zr * 2 + cr))
        ids_ref[0, pl.ds(at * rows, rows), :] = idx_ref[0, pl.ds(block * rows, rows), :] - first
        val_scr[pl.ds(at * rows, rows), :] = val_ref[0, pl.ds(block * rows, rows), :]
        return 0

    lax.fori_loop(0, tokens // rows, run, 0)


def build_acts(ids_ref, val_scr, acts_ref, rows_scr, hi_scr, lo_scr, vhi_scr, vlo_scr, span):
    _, tokens, active = ids_ref.shape
    blocks = acts_ref.shape[-1] // LANES
    pitch = 2 * blocks + 1
    iota_block = lax.broadcasted_iota(i32, (blocks, active), 0)
    iota_lane = lax.broadcasted_iota(i32, (LANES, active), 0)
    ids = ids_ref[0]
    vhi, vlo = split(val_scr[...])
    hi_scr[...] = ids >> 7
    lo_scr[...] = ids & 127
    vhi_scr[...] = vhi.astype(f32)
    vlo_scr[...] = vlo.astype(f32)
    empty = jnp.zeros((2 * blocks, active), bf16)

    def factors(at):
        def row(ref, count):
            return jnp.broadcast_to(ref[pl.ds(at, 1), :], (count, active))

        hit = row(hi_scr, blocks) == iota_block
        high = jnp.where(hit, row(vhi_scr, blocks), 0.0)
        low = jnp.where(hit, row(vlo_scr, blocks), 0.0)
        weights = jnp.concatenate([high, low], axis=0).astype(bf16)
        onehot = jnp.where(row(lo_scr, LANES) == iota_lane, 1.0, 0.0).astype(bf16)
        return weights, onehot

    def part(b, _):
        base = pl.multiple_of(b * span, span)
        for i in range(0, span, 2):
            w0, o0 = factors(base + i)
            w1, o1 = factors(base + i + 1)
            weights = jnp.concatenate(
                [jnp.concatenate([w0, empty], axis=1), jnp.concatenate([empty, w1], axis=1)], axis=0
            )
            onehot = jnp.concatenate([o0, o1], axis=1)
            got = lax.dot_general(weights, onehot, NT, preferred_element_type=f32)
            rows_scr[i * pitch:i * pitch + 2 * blocks, :] = got[:2 * blocks]
            rows_scr[(i + 1) * pitch:(i + 1) * pitch + 2 * blocks, :] = got[2 * blocks:]
        for h in range(blocks):
            lanes = slice(h * LANES, (h + 1) * LANES)
            high = rows_scr[pl.ds(h, span, stride=pitch), :]
            low = rows_scr[pl.ds(blocks + h, span, stride=pitch), :]
            acts_ref[0, pl.ds(base, span), lanes] = high.astype(bf16)
            acts_ref[0, pl.ds(tokens + base, span), lanes] = low.astype(bf16)
        return 0

    lax.fori_loop(0, tokens // span, part, 0)


def recon_kernel(pairs, zs, span, map_ref, idx_ref, val_ref, dec_ref, keep_ref, send_ref, acts_ref, ids_ref, val_scr, *scr):
    @pl.when(pl.program_id(1) == 0)
    def _():
        lay_out(acts_ref.shape[-1], idx_ref, val_ref, ids_ref, val_scr, pairs, zs)
        build_acts(ids_ref, val_scr, acts_ref, *scr, span)

    tokens = idx_ref.shape[1]
    dhi, dlo = split(dec_ref[0])
    both = jnp.dot(acts_ref[0], dhi, preferred_element_type=f32)
    low = jnp.dot(acts_ref[0, :tokens], dlo, preferred_element_type=f32)
    prod = both[:tokens] + both[tokens:] + low
    keep_ref[0] = prod[:tokens // 2]
    send_ref[0] = prod[tokens // 2:]


def recon_call(pair_map, indices, values, decoder, pairs, zs, tile=512, span=64):
    slots, features, width = decoder.shape
    layers, tokens, active = indices.shape
    tile = min(tile, width)
    blocks = features // LANES
    layer = pl.BlockSpec((1, tokens, active), lambda j, n, m: (jnp.minimum(m[j, 0], layers - 1), 0, 0))
    half = pl.BlockSpec((1, tokens // 2, tile), lambda j, n, m: (j, 0, n))

    def kernel(*refs):
        recon_kernel(pairs, zs, span, *refs)

    def slot(rows, cols):
        return pl.BlockSpec((1, rows, cols), lambda j, n, m: (j, 0, 0))

    return pl.pallas_call(
        kernel,
        out_shape=(
            jax.ShapeDtypeStruct((slots, tokens // 2, width), f32),
            jax.ShapeDtypeStruct((slots, tokens // 2, width), f32),
            jax.ShapeDtypeStruct((slots, 2 * tokens, features), bf16),
            jax.ShapeDtypeStruct((slots, tokens, active), i32),
        ),
        grid_spec=pltpu.PrefetchScalarGridSpec(
            num_scalar_prefetch=1,
            grid=(slots, width // tile),
            in_specs=[layer, layer, pl.BlockSpec((1, features, tile), lambda j, n, m: (j, 0, n))],
            out_specs=[half, half, slot(2 * tokens, features), slot(tokens, active)],
            scratch_shapes=[
                pltpu.VMEM((tokens, active), f32),
                pltpu.VMEM((span * (2 * blocks + 1) + 8, LANES), f32),
                pltpu.VMEM((tokens, active), i32),
                pltpu.VMEM((tokens, active), i32),
                pltpu.VMEM((tokens, active), f32),
                pltpu.VMEM((tokens, active), f32),
            ],
        ),
        compiler_params=params(),
        cost_estimate=cost(6 * slots * tokens * features * width, 4 * slots * features * width),
        name="recon",
    )(pair_map, indices, values, decoder)


def gather_errors(pieces, err_scr):
    at = 0
    for piece in pieces:
        rows = piece.shape[1]
        err_scr[at:at + rows] = piece[0]
        at += rows


def back_kernel(count, ids_ref, *refs):
    pieces, (dec_ref, keep_ref, send_ref, out_ref, err_scr) = refs[:count], refs[count:]
    n = pl.program_id(1)
    depth = dec_ref.shape[1]

    @pl.when(n == 0)
    def _():
        out_ref[...] = jnp.zeros_like(out_ref)
        gather_errors(pieces, err_scr)

    dhi, dlo = split(dec_ref[0])
    err = err_scr[...]
    grad = lax.dot_general(err, dhi, NT, preferred_element_type=f32)
    grad += lax.dot_general(err, dlo, NT, preferred_element_type=f32)
    ids = ids_ref[0] - n * depth
    block = ids >> 7
    lane = ids & 127
    total = out_ref[...]
    for c in range(depth // LANES):
        picked = jnp.take_along_axis(grad[:, c * LANES:(c + 1) * LANES], lane, axis=1)
        total = jnp.where(block == c, picked, total)
    out_ref[...] = total

    @pl.when(n == pl.num_programs(1) - 1)
    def _():
        half = total.shape[0] // 2
        keep_ref[0] = total[:half]
        send_ref[0] = total[half:]


def back_call(ids, pieces, decoder, depth=512):
    slots, features, width = decoder.shape
    _, tokens, active = ids.shape
    depth = min(depth, features)

    def kernel(*refs):
        back_kernel(len(pieces), *refs)

    return pl.pallas_call(
        kernel,
        out_shape=[jax.ShapeDtypeStruct((slots, tokens // 2, active), f32)] * 2,
        grid=(slots, features // depth),
        in_specs=[pl.BlockSpec((1, tokens, active), lambda j, n: (j, 0, 0))]
        + [pl.BlockSpec((1, x.shape[1], width), lambda j, n: (j, 0, 0)) for x in pieces]
        + [pl.BlockSpec((1, depth, width), lambda j, n: (j, n, 0))],
        out_specs=[pl.BlockSpec((1, tokens // 2, active), lambda j, n: (j, 0, 0))] * 2,
        scratch_shapes=[pltpu.VMEM((tokens, active), f32), pltpu.VMEM((tokens, width), bf16)],
        compiler_params=params(),
        cost_estimate=cost(4 * slots * tokens * features * width, 4 * slots * features * width),
        name="back",
    )(ids, *pieces, decoder)


def grad_kernel(count, acts_ref, *refs):
    pieces, (out_ref, err_scr) = refs[:count], refs[-2:]
    tokens = err_scr.shape[0] // 2

    @pl.when(pl.program_id(0) == 0)
    def _():
        gather_errors(pieces, err_scr)
        err_scr[tokens:] = err_scr[:tokens]

    out_ref[0] = lax.dot_general(acts_ref[0], err_scr[...], TN, preferred_element_type=f32)


def grad_call(acts, pieces, slot, earlier, depth=512):
    slots, rows, features = acts.shape
    width = pieces[0].shape[2]
    depth = min(depth, features)
    count = len(pieces)

    def kernel(*refs):
        grad_kernel(count, *refs)

    more = [] if earlier is None else [earlier]
    return pl.pallas_call(
        kernel,
        out_shape=jax.ShapeDtypeStruct((slots, features, width), f32),
        grid=(features // depth,),
        in_specs=[pl.BlockSpec((1, rows, depth), lambda n: (slot, 0, n))]
        + [pl.BlockSpec((1, x.shape[1], width), lambda n: (slot, 0, 0)) for x in pieces]
        + [pl.BlockSpec(memory_space=pl.ANY)] * len(more),
        out_specs=pl.BlockSpec((1, depth, width), lambda n: (slot, n, 0)),
        scratch_shapes=[pltpu.VMEM((rows, width), bf16)],
        input_output_aliases={count + 1: 0} if more else {},
        compiler_params=params(),
        cost_estimate=cost(2 * rows * features * width, 4 * features * width),
        name="grad",
    )(acts, *pieces, *more)


def layer_sums(tables, blocks, layers):
    shape = blocks[0].shape[1:]

    def kernel(table_ref, *refs):
        out_ref = refs[-1]
        out_ref[...] = jnp.zeros_like(out_ref)
        for m, ref in enumerate(refs[:-1]):
            for j in range(ref.shape[0]):
                goal = table_ref[m, j]

                @pl.when(goal < layers)
                def _():
                    out_ref[goal] = out_ref[goal] + ref[j]

    return pl.pallas_call(
        kernel,
        out_shape=jax.ShapeDtypeStruct((layers,) + shape, f32),
        in_specs=[pl.BlockSpec(memory_space=pltpu.SMEM)] + [pl.BlockSpec(memory_space=pltpu.VMEM)] * len(blocks),
        out_specs=pl.BlockSpec(memory_space=pltpu.VMEM),
        compiler_params=params(),
        name="layer_sums",
    )(jnp.stack(tables), *blocks)


def choose_layers(tables, errors, slots):
    layers, rows, width = errors[0].shape
    if rows % 8:
        column = jnp.concatenate(errors, axis=1)
        out = []
        for table in tables:
            picked = [
                sum(jnp.where(table[j] == layer, column[layer], jnp.zeros((), bf16)) for layer in range(layers))
                for j in range(slots)
            ]
            out.append(jnp.stack(picked))
        return out
    count = len(tables)
    total = len(errors) * rows

    def kernel(table_ref, *refs):
        for m, out_ref in enumerate(refs[len(errors):]):
            for j in range(slots):
                goal = table_ref[m, j]
                at = jnp.minimum(goal, layers - 1)
                live = jnp.where(goal < layers, 1.0, 0.0)
                wide = jnp.concatenate([ref[at].astype(f32) for ref in refs[:len(errors)]], axis=0)
                out_ref[j] = (wide * live).astype(bf16)

    return pl.pallas_call(
        kernel,
        out_shape=[jax.ShapeDtypeStruct((slots, total, width), bf16)] * count,
        in_specs=[pl.BlockSpec(memory_space=pltpu.SMEM)] + [pl.BlockSpec(memory_space=pltpu.VMEM)] * len(errors),
        out_specs=[pl.BlockSpec(memory_space=pltpu.VMEM)] * count,
        compiler_params=params(),
        name="choose_layers",
    )(jnp.stack(tables), *errors)


def swap_cores(x):
    return lax.ppermute(x, "feat", [(i, i ^ 1) for i in range(lax.axis_size("feat"))])


def swap_z(x, m):
    return lax.ppermute(x, "feat", [(i, i ^ (2 * m)) for i in range(lax.axis_size("feat"))])


def swap_pair(x, m):
    return lax.ppermute(x, "pair", [(i, i ^ m) for i in range(lax.axis_size("pair"))])


def pack(x):
    return (x * WIRE_SCALE).astype(jnp.float16)


def unpack(x):
    return x.astype(f32) * (1.0 / WIRE_SCALE)


def weigh(tables, blocks, layers):
    total = 0.0
    for table, block in zip(tables, blocks):
        for j in range(block.shape[0]):
            chosen = (jnp.arange(layers, dtype=i32) == table[j]).astype(f32)
            total = total + chosen[:, None, None] * block[j][None]
    return total


def sum_full(keep, send, pair_map, layers):
    pairs, zs = lax.axis_size("pair"), lax.axis_size("feat") // 2
    run = keep.shape[1] // pairs
    rows = run // zs
    got = swap_cores(send)
    halves = [keep[:, m * run:(m + 1) * run] + got[:, m * run:(m + 1) * run] for m in range(pairs)]
    packed = [pack(x) for x in halves[1:]]
    arrived = [None] + [swap_pair(packed[m - 1], m) for m in range(1, pairs)]
    pair_map, _ = lax.optimization_barrier((pair_map, packed[0]))
    maps = [pair_map] + [swap_pair(pair_map, m) for m in range(1, pairs)]
    sources = [x[:, 0] for x in maps]
    goals = [x[:, 1] for x in maps]
    parts = []
    for k in range(zs):
        cut = slice(k * rows, (k + 1) * rows)
        blocks = [halves[0][:, cut]] + [unpack(x[:, cut]) for x in arrived[1:]]
        parts.append(weigh(goals, blocks, layers))
    sent = [pack(x) for x in parts[1:]]
    full = parts[0]
    for m in range(1, zs):
        full = full + unpack(swap_z(sent[m - 1], m))
    return full, sources, goals


def spread_errors(error, goals, slots):
    pairs, zs = lax.axis_size("pair"), lax.axis_size("feat") // 2
    errors = [error] + [swap_z(error, m) for m in range(1, zs)]
    chosen = choose_layers(goals, errors, slots)
    own = [chosen[0]] + [swap_pair(chosen[m], m) for m in range(1, pairs)]
    return own + [swap_cores(x) for x in own]


def finish(keep, send, sources, layers, acts, pieces):
    pairs, zs = lax.axis_size("pair"), lax.axis_size("feat") // 2
    slots, half_rows, width = keep.shape
    rows = half_rows // (pairs * zs)
    half = (keep + swap_cores(send)).reshape(slots, pairs, zs, rows, width)
    arrived = [half[:, :, 0]] + [swap_z(half[:, :, m], m) for m in range(1, zs)]
    dec_grad = None
    for j in range(0, slots - 1):
        dec_grad = grad_call(acts, pieces, j, dec_grad)
    if dec_grad is not None:
        dec_grad, *arrived = lax.optimization_barrier((dec_grad, *arrived))
    column = sum(arrived)
    arrived = [column[:, 0]] + [swap_pair(column[:, m], m) for m in range(1, pairs)]
    dec_grad = grad_call(acts, pieces, slots - 1, dec_grad)
    dec_grad, *arrived = lax.optimization_barrier((dec_grad, *arrived))
    return dec_grad, layer_sums(sources, arrived, layers)


def body(decoder, pair_map, indices, values, target):
    slots = decoder.shape[0]
    layers = indices.shape[0]
    pairs, zs = lax.axis_size("pair"), lax.axis_size("feat") // 2
    keep, send, acts, ids = recon_call(pair_map, indices, values, decoder, pairs, zs)
    full, sources, goals = sum_full(keep, send, pair_map, layers)
    recon = full.astype(bf16)
    error = (full - target).astype(bf16)
    pieces = spread_errors(error, goals, slots)
    keep, send = back_call(ids, pieces, decoder)
    dec_grad, feat_grad = finish(keep, send, sources, layers, acts, pieces)
    return recon, dec_grad, feat_grad


def solution(mesh):
    in_specs = (P("pair", "feat", None), P("pair", None), P(), P(), P(None, ("pair", "feat"), None))
    out_specs = (
        P(None, ("pair", "feat"), None),
        P("pair", "feat", None),
        P(None, ("pair", "feat"), None),
    )
    return jax.shard_map(body, mesh=mesh, in_specs=in_specs, out_specs=out_specs, check_vma=False)
```

```python
import jax
import jax.numpy as jnp
from jax import lax
from jax.experimental import pallas as pl
from jax.experimental.pallas import tpu as pltpu
from jax.sharding import PartitionSpec as P

f32 = jnp.float32
bf16 = jnp.bfloat16
i32 = jnp.int32
LANES = 128
WIRE_SCALE = 128.0
VMEM_LIMIT = 56 << 20
BACK_DEPTH = 1024
NT = (((1,), (1,)), ((), ()))
TN = (((0,), (0,)), ((), ()))


def split(x):
    hi = x.astype(bf16)
    return hi, (x - hi.astype(f32)).astype(bf16)


def cost(flops, nbytes):
    return pl.CostEstimate(flops=int(flops), bytes_accessed=int(nbytes), transcendentals=0)


def params():
    return pltpu.CompilerParams(vmem_limit_bytes=VMEM_LIMIT)


def lay_out(features, idx_ref, val_ref, ids_ref, val_scr, pairs, zs):
    tokens = idx_ref.shape[1]
    rows = tokens // (pairs * zs * 2)
    p, feat = lax.axis_index("pair"), lax.axis_index("feat")
    first = feat * features

    def run(at, _):
        zr = at & (zs - 1)
        pr = (at // zs) & (pairs - 1)
        cr = at // (zs * pairs)
        block = (p ^ pr) * (zs * 2) + (feat ^ (zr * 2 + cr))
        ids_ref[0, pl.ds(at * rows, rows), :] = idx_ref[0, pl.ds(block * rows, rows), :] - first
        val_scr[pl.ds(at * rows, rows), :] = val_ref[0, pl.ds(block * rows, rows), :]
        return 0

    lax.fori_loop(0, tokens // rows, run, 0)


def build_acts(ids_ref, val_scr, acts_ref, rows_scr, hi_scr, lo_scr, vhi_scr, vlo_scr, span):
    _, tokens, active = ids_ref.shape
    blocks = acts_ref.shape[-1] // LANES
    pitch = 2 * blocks + 1
    iota_block = lax.broadcasted_iota(i32, (blocks, active), 0)
    iota_lane = lax.broadcasted_iota(i32, (LANES, active), 0)
    ids = ids_ref[0]
    vhi, vlo = split(val_scr[...])
    hi_scr[...] = ids >> 7
    lo_scr[...] = ids & 127
    vhi_scr[...] = vhi.astype(f32)
    vlo_scr[...] = vlo.astype(f32)
    empty = jnp.zeros((2 * blocks, active), bf16)

    def factors(at):
        def row(ref, count):
            return jnp.broadcast_to(ref[pl.ds(at, 1), :], (count, active))

        hit = row(hi_scr, blocks) == iota_block
        high = jnp.where(hit, row(vhi_scr, blocks), 0.0)
        low = jnp.where(hit, row(vlo_scr, blocks), 0.0)
        weights = jnp.concatenate([high, low], axis=0).astype(bf16)
        onehot = jnp.where(row(lo_scr, LANES) == iota_lane, 1.0, 0.0).astype(bf16)
        return weights, onehot

    def part(b, _):
        base = pl.multiple_of(b * span, span)
        for i in range(0, span, 2):
            w0, o0 = factors(base + i)
            w1, o1 = factors(base + i + 1)
            weights = jnp.concatenate(
                [jnp.concatenate([w0, empty], axis=1), jnp.concatenate([empty, w1], axis=1)], axis=0
            )
            onehot = jnp.concatenate([o0, o1], axis=1)
            got = lax.dot_general(weights, onehot, NT, preferred_element_type=f32)
            rows_scr[i * pitch:i * pitch + 2 * blocks, :] = got[:2 * blocks]
            rows_scr[(i + 1) * pitch:(i + 1) * pitch + 2 * blocks, :] = got[2 * blocks:]
        for h in range(blocks):
            lanes = slice(h * LANES, (h + 1) * LANES)
            high = rows_scr[pl.ds(h, span, stride=pitch), :]
            low = rows_scr[pl.ds(blocks + h, span, stride=pitch), :]
            acts_ref[0, pl.ds(base, span), lanes] = high.astype(bf16)
            acts_ref[0, pl.ds(tokens + base, span), lanes] = low.astype(bf16)
        return 0

    lax.fori_loop(0, tokens // span, part, 0)


def recon_kernel(pairs, zs, span, map_ref, idx_ref, val_ref, dec_ref, keep_ref, send_ref, acts_ref, ids_ref, val_scr, *scr):
    @pl.when(pl.program_id(1) == 0)
    def _():
        lay_out(acts_ref.shape[-1], idx_ref, val_ref, ids_ref, val_scr, pairs, zs)
        build_acts(ids_ref, val_scr, acts_ref, *scr, span)

    tokens = idx_ref.shape[1]
    dhi, dlo = split(dec_ref[0])
    both = jnp.dot(acts_ref[0], dhi, preferred_element_type=f32)
    low = jnp.dot(acts_ref[0, :tokens], dlo, preferred_element_type=f32)
    prod = both[:tokens] + both[tokens:] + low
    keep_ref[0] = prod[:tokens // 2]
    send_ref[0] = prod[tokens // 2:]


def recon_call(pair_map, indices, values, decoder, pairs, zs, tile=1024, span=64):
    slots, features, width = decoder.shape
    layers, tokens, active = indices.shape
    tile = min(tile, width)
    blocks = features // LANES
    layer = pl.BlockSpec((1, tokens, active), lambda j, n, m: (jnp.minimum(m[j, 0], layers - 1), 0, 0))
    half = pl.BlockSpec((1, tokens // 2, tile), lambda j, n, m: (j, 0, n))

    def kernel(*refs):
        recon_kernel(pairs, zs, span, *refs)

    def slot(rows, cols):
        return pl.BlockSpec((1, rows, cols), lambda j, n, m: (j, 0, 0))

    return pl.pallas_call(
        kernel,
        out_shape=(
            jax.ShapeDtypeStruct((slots, tokens // 2, width), f32),
            jax.ShapeDtypeStruct((slots, tokens // 2, width), f32),
            jax.ShapeDtypeStruct((slots, 2 * tokens, features), bf16),
            jax.ShapeDtypeStruct((slots, tokens, active), i32),
        ),
        grid_spec=pltpu.PrefetchScalarGridSpec(
            num_scalar_prefetch=1,
            grid=(slots, width // tile),
            in_specs=[layer, layer, pl.BlockSpec((1, features, tile), lambda j, n, m: (j, 0, n))],
            out_specs=[half, half, slot(2 * tokens, features), slot(tokens, active)],
            scratch_shapes=[
                pltpu.VMEM((tokens, active), f32),
                pltpu.VMEM((span * (2 * blocks + 1) + 8, LANES), f32),
                pltpu.VMEM((tokens, active), i32),
                pltpu.VMEM((tokens, active), i32),
                pltpu.VMEM((tokens, active), f32),
                pltpu.VMEM((tokens, active), f32),
            ],
        ),
        compiler_params=params(),
        cost_estimate=cost(6 * slots * tokens * features * width, 4 * slots * features * width),
        name="recon",
    )(pair_map, indices, values, decoder)


def gather_errors(pieces, err_scr):
    for j in range(err_scr.shape[0]):
        at = 0
        for piece in pieces:
            rows = piece.shape[1]
            err_scr[j, at:at + rows] = piece[j]
            at += rows


def acts_grad(acts_ref, err):
    return lax.dot_general(acts_ref[0], err, TN, preferred_element_type=f32)


def back_kernel(count, slot_steps, ids_ref, acts_ref, dec_ref, *refs):
    pieces, (keep_ref, send_ref, grad_ref, total_scr, err_scr) = refs[:count], refs[count:]
    i = pl.program_id(0)
    j, n = i // slot_steps, lax.rem(i, slot_steps)
    depth, grad_depth = dec_ref.shape[1], grad_ref.shape[1]

    @pl.when(i == 0)
    def _():
        gather_errors(pieces, err_scr)

    @pl.when(n == 0)
    def _():
        total_scr[...] = jnp.zeros_like(total_scr)

    back = lax.dot_general(err_scr[j], dec_ref[0].astype(bf16), NT, preferred_element_type=f32)
    grad_ref[0] = acts_grad(acts_ref, err_scr[i * grad_depth // (slot_steps * depth)])
    ids = ids_ref[0] - n * depth
    block = ids >> 7
    lane = ids & 127
    total = total_scr[...]
    for c in range(depth // LANES):
        picked = jnp.take_along_axis(back[:, c * LANES:(c + 1) * LANES], lane, axis=1)
        total = jnp.where(block == c, picked, total)
    total_scr[...] = total

    @pl.when(n == slot_steps - 1)
    def _():
        half = total.shape[0] // 2
        keep_ref[0] = total[:half]
        send_ref[0] = total[half:]


def back_call(ids, acts, pieces, decoder, depth=BACK_DEPTH):
    slots, features, width = decoder.shape
    _, tokens, active = ids.shape
    depth = min(depth, features)
    grad_depth = depth // 2
    slot_steps = features // depth
    slot_parts = features // grad_depth
    count = len(pieces)

    def kernel(*refs):
        back_kernel(count, slot_steps, *refs)

    half = pl.BlockSpec((1, tokens // 2, active), lambda i: (i // slot_steps, 0, 0))
    return pl.pallas_call(
        kernel,
        out_shape=[jax.ShapeDtypeStruct((slots, tokens // 2, active), f32)] * 2
        + [jax.ShapeDtypeStruct((slots, features, width), f32)],
        grid=(slots * slot_steps,),
        in_specs=[
            pl.BlockSpec((1, tokens, active), lambda i: (i // slot_steps, 0, 0)),
            pl.BlockSpec((1, tokens, grad_depth), lambda i: (i // slot_parts, 0, i % slot_parts)),
            pl.BlockSpec((1, depth, width), lambda i: (i // slot_steps, i % slot_steps, 0)),
        ]
        + [pl.BlockSpec(x.shape, lambda i: (0, 0, 0)) for x in pieces],
        out_specs=[half, half, pl.BlockSpec((1, grad_depth, width), lambda i: (i // slot_parts, i % slot_parts, 0))],
        scratch_shapes=[pltpu.VMEM((tokens, active), f32), pltpu.VMEM((slots, tokens, width), bf16)],
        compiler_params=params(),
        cost_estimate=cost(3 * slots * tokens * features * width, 6 * slots * features * width),
        name="back",
    )(ids, acts, decoder, *pieces)


def grad_kernel(count, acts_ref, *refs):
    pieces, (grad_ref, err_scr) = refs[:count], refs[-2:]

    @pl.when(pl.program_id(0) == 0)
    def _():
        gather_errors(pieces, err_scr)

    grad_ref[0] = acts_grad(acts_ref, err_scr[0])


def grad_call(acts, pieces, quarter, earlier, depth=512):
    slots, rows, features = acts.shape
    tokens = rows // 2
    width = pieces[0].shape[2]
    span = slots * features // 4
    slot, first = quarter * span // features, quarter * span % features
    depth = min(depth, span)
    count = len(pieces)

    def kernel(*refs):
        grad_kernel(count, *refs)

    return pl.pallas_call(
        kernel,
        out_shape=jax.ShapeDtypeStruct((slots, features, width), f32),
        grid=(span // depth,),
        in_specs=[pl.BlockSpec((1, tokens, depth), lambda i: (slot, 0, first // depth + i))]
        + [pl.BlockSpec((1, x.shape[1], width), lambda i: (slot, 0, 0)) for x in pieces]
        + [pl.BlockSpec(memory_space=pl.ANY)],
        out_specs=pl.BlockSpec((1, depth, width), lambda i: (slot, first // depth + i, 0)),
        scratch_shapes=[pltpu.VMEM((1, tokens, width), bf16)],
        input_output_aliases={count + 1: 0},
        compiler_params=params(),
        cost_estimate=cost(2 * span * tokens * width, 4 * span * width),
        name="grad",
    )(acts, *pieces, earlier)


def layer_sums(tables, blocks, layers):
    shape = blocks[0].shape[1:]

    def kernel(table_ref, *refs):
        out_ref = refs[-1]
        out_ref[...] = jnp.zeros_like(out_ref)
        for m, ref in enumerate(refs[:-1]):
            for j in range(ref.shape[0]):
                goal = table_ref[m, j]

                @pl.when(goal < layers)
                def _():
                    out_ref[goal] = out_ref[goal] + ref[j]

    return pl.pallas_call(
        kernel,
        out_shape=jax.ShapeDtypeStruct((layers,) + shape, f32),
        in_specs=[pl.BlockSpec(memory_space=pltpu.SMEM)] + [pl.BlockSpec(memory_space=pltpu.VMEM)] * len(blocks),
        out_specs=pl.BlockSpec(memory_space=pltpu.VMEM),
        compiler_params=params(),
        name="layer_sums",
    )(tables, *blocks)


def choose_layers(tables, errors, slots):
    layers, rows, width = errors[0].shape
    if rows % 8:
        column = jnp.concatenate(errors, axis=1)
        out = []
        for table in tables:
            picked = [
                sum(jnp.where(table[j] == layer, column[layer], jnp.zeros((), bf16)) for layer in range(layers))
                for j in range(slots)
            ]
            out.append(jnp.stack(picked))
        return out
    count = tables.shape[0]
    total = len(errors) * rows

    def kernel(table_ref, *refs):
        for m, out_ref in enumerate(refs[len(errors):]):
            for j in range(slots):
                goal = table_ref[m, j]
                at = jnp.minimum(goal, layers - 1)
                live = jnp.where(goal < layers, 1.0, 0.0)
                wide = jnp.concatenate([ref[at].astype(f32) for ref in refs[:len(errors)]], axis=0)
                out_ref[j] = (wide * live).astype(bf16)

    return pl.pallas_call(
        kernel,
        out_shape=[jax.ShapeDtypeStruct((slots, total, width), bf16)] * count,
        in_specs=[pl.BlockSpec(memory_space=pltpu.SMEM)] + [pl.BlockSpec(memory_space=pltpu.VMEM)] * len(errors),
        out_specs=[pl.BlockSpec(memory_space=pltpu.VMEM)] * count,
        compiler_params=params(),
        name="choose_layers",
    )(tables, *errors)


def swap_cores(x):
    return lax.ppermute(x, "feat", [(i, i ^ 1) for i in range(lax.axis_size("feat"))])


def swap_z(x, m):
    return lax.ppermute(x, "feat", [(i, i ^ (2 * m)) for i in range(lax.axis_size("feat"))])


def swap_pair(x, m):
    return lax.ppermute(x, "pair", [(i, i ^ m) for i in range(lax.axis_size("pair"))])


def pack(x):
    return (x * WIRE_SCALE).astype(jnp.float16)


def unpack(x):
    return x.astype(f32) * (1.0 / WIRE_SCALE)


def weigh(chosen, blocks):
    total = 0.0
    for m, block in enumerate(blocks):
        for j in range(block.shape[0]):
            total = total + chosen[m, j][:, None, None] * block[j][None]
    return total


def sum_full(keep, send, pair_map, layers):
    pairs, zs = lax.axis_size("pair"), lax.axis_size("feat") // 2
    run = keep.shape[1] // pairs
    rows = run // zs
    got = swap_cores(send)
    pair_map, _ = lax.optimization_barrier((pair_map, keep))
    maps = [pair_map] + [swap_pair(pair_map, m) for m in range(1, pairs)]
    halves = [keep[:, m * run:(m + 1) * run] + got[:, m * run:(m + 1) * run] for m in range(pairs)]
    packed = [pack(x) for x in halves[1:]]
    arrived = [None] + [swap_pair(packed[m - 1], m) for m in range(1, pairs)]
    maps, _ = lax.optimization_barrier((jnp.stack(maps), packed))
    sources, goals = maps[:, :, 0], maps[:, :, 1]
    chosen = (goals[:, :, None] == jnp.arange(layers, dtype=i32)).astype(f32)
    chosen, sources, goals = lax.optimization_barrier((chosen, sources, goals))
    parts = []
    for k in range(zs):
        cut = slice(k * rows, (k + 1) * rows)
        blocks = [halves[0][:, cut]] + [unpack(x[:, cut]) for x in arrived[1:]]
        parts.append(weigh(chosen, blocks))
    sent = [pack(x) for x in parts[1:]]
    full = parts[0]
    for m in range(1, zs):
        full = full + unpack(swap_z(sent[m - 1], m))
    return full, sources, goals


def spread_errors(error, goals, slots):
    pairs, zs = lax.axis_size("pair"), lax.axis_size("feat") // 2
    errors = [error] + [swap_z(error, m) for m in range(1, zs)]
    chosen = choose_layers(goals, errors, slots)
    own = [chosen[0]] + [swap_pair(chosen[m], m) for m in range(1, pairs)]
    return own + [swap_cores(x) for x in own]


def finish(keep, send, sources, layers, acts, pieces, dec_grad):
    pairs, zs = lax.axis_size("pair"), lax.axis_size("feat") // 2
    slots, half_rows, width = keep.shape
    rows = half_rows // (pairs * zs)
    half = (keep + swap_cores(send)).reshape(slots, pairs, zs, rows, width)
    arrived = [half[:, :, 0]] + [swap_z(half[:, :, m], m) for m in range(1, zs)]
    dec_grad = grad_call(acts, pieces, 2, dec_grad)
    dec_grad, *arrived = lax.optimization_barrier((dec_grad, *arrived))
    column = sum(arrived)
    arrived = [column[:, 0]] + [swap_pair(column[:, m], m) for m in range(1, pairs)]
    dec_grad = grad_call(acts, pieces, 3, dec_grad)
    dec_grad, *arrived = lax.optimization_barrier((dec_grad, *arrived))
    return dec_grad, layer_sums(sources, arrived, layers)


def body(decoder, pair_map, indices, values, target):
    slots = decoder.shape[0]
    layers = indices.shape[0]
    pairs, zs = lax.axis_size("pair"), lax.axis_size("feat") // 2
    keep, send, acts, ids = recon_call(pair_map, indices, values, decoder, pairs, zs)
    full, sources, goals = sum_full(keep, send, pair_map, layers)
    recon = full.astype(bf16)
    error = (full - target).astype(bf16)
    pieces = spread_errors(error, goals, slots)
    keep, send, dec_grad = back_call(ids, acts, pieces, decoder)
    dec_grad, feat_grad = finish(keep, send, sources, layers, acts, pieces, dec_grad)
    return recon, dec_grad, feat_grad


def solution(mesh):
    in_specs = (P("pair", "feat", None), P("pair", None), P(), P(), P(None, ("pair", "feat"), None))
    out_specs = (
        P(None, ("pair", "feat"), None),
        P("pair", "feat", None),
        P(None, ("pair", "feat"), None),
    )
    return jax.shard_map(body, mesh=mesh, in_specs=in_specs, out_specs=out_specs, check_vma=False)
```

```python
import jax
import jax.numpy as jnp
from jax import lax
from jax.experimental import pallas as pl
from jax.experimental.pallas import tpu as pltpu
from jax.sharding import PartitionSpec as P

f32 = jnp.float32
bf16 = jnp.bfloat16
i32 = jnp.int32
LANES = 128
WIRE_SCALE = 128.0
BACK_DEPTH = 1024
RECON_TILE = 512
NT = (((1,), (1,)), ((), ()))
TN = (((0,), (0,)), ((), ()))


def split(x):
    hi = x.astype(bf16)
    return hi, (x - hi.astype(f32)).astype(bf16)


def cost(flops, nbytes):
    return pl.CostEstimate(flops=int(flops), bytes_accessed=int(nbytes), transcendentals=0)


def params(mib):
    return pltpu.CompilerParams(vmem_limit_bytes=mib << 20)


def prepare(slot, layer, refs, pairs, zs, features):
    idx_ref, val_ref, ids_ref, val_scr, hi_scr, lo_scr, vhi_scr, vlo_scr = refs
    tokens = idx_ref.shape[1]
    rows = tokens // (pairs * zs * 2)
    p, feat = lax.axis_index("pair"), lax.axis_index("feat")
    first = feat * features

    def run(at, _):
        zr = at & (zs - 1)
        pr = (at // zs) & (pairs - 1)
        cr = at // (zs * pairs)
        block = (p ^ pr) * (zs * 2) + (feat ^ (zr * 2 + cr))
        ids_ref[slot, pl.ds(at * rows, rows), :] = idx_ref[layer, pl.ds(block * rows, rows), :] - first
        val_scr[pl.ds(at * rows, rows), :] = val_ref[layer, pl.ds(block * rows, rows), :]
        return 0

    lax.fori_loop(0, tokens // rows, run, 0)
    ids = ids_ref[slot]
    vhi, vlo = split(val_scr[...])
    hi_scr[...] = ids >> 7
    lo_scr[...] = ids & 127
    vhi_scr[...] = vhi.astype(f32)
    vlo_scr[...] = vlo.astype(f32)


def build_span(part, span, high_ref, low_ref, rows_scr, hi_scr, lo_scr, vhi_scr, vlo_scr):
    active = hi_scr.shape[1]
    blocks = high_ref.shape[-1] // LANES
    pitch = 2 * blocks + 1
    iota_block = lax.broadcasted_iota(i32, (blocks, active), 0)
    iota_lane = lax.broadcasted_iota(i32, (LANES, active), 0)
    empty = jnp.zeros((2 * blocks, active), bf16)
    base = pl.multiple_of(part * span, span)

    def factors(at):
        def row(ref, count):
            return jnp.broadcast_to(ref[pl.ds(at, 1), :], (count, active))

        hit = row(hi_scr, blocks) == iota_block
        high = jnp.where(hit, row(vhi_scr, blocks), 0.0)
        low = jnp.where(hit, row(vlo_scr, blocks), 0.0)
        weights = jnp.concatenate([high, low], axis=0).astype(bf16)
        onehot = jnp.where(row(lo_scr, LANES) == iota_lane, 1.0, 0.0).astype(bf16)
        return weights, onehot

    for i in range(0, span, 2):
        w0, o0 = factors(base + i)
        w1, o1 = factors(base + i + 1)
        weights = jnp.concatenate(
            [jnp.concatenate([w0, empty], axis=1), jnp.concatenate([empty, w1], axis=1)], axis=0
        )
        onehot = jnp.concatenate([o0, o1], axis=1)
        got = lax.dot_general(weights, onehot, NT, preferred_element_type=f32)
        rows_scr[i * pitch:i * pitch + 2 * blocks, :] = got[:2 * blocks]
        rows_scr[(i + 1) * pitch:(i + 1) * pitch + 2 * blocks, :] = got[2 * blocks:]
    for h in range(blocks):
        lanes = slice(h * LANES, (h + 1) * LANES)
        high = rows_scr[pl.ds(h, span, stride=pitch), :]
        low = rows_scr[pl.ds(blocks + h, span, stride=pitch), :]
        high_ref[pl.ds(base, span), lanes] = high.astype(bf16)
        low_ref[pl.ds(base, span), lanes] = low.astype(bf16)


def recon_kernel(slots, layers, pairs, zs, span, map_ref, idx_ref, val_ref, dec_ref, keep_ref, send_ref, acts_ref, ids_ref, *scr):
    lows, (rows_scr, val_scr, *split_scr) = scr[:slots], scr[slots:]
    _, tokens, features = acts_ref.shape
    j, n = pl.program_id(0), pl.program_id(1)
    steps = tokens // span
    share = -(-steps // pl.num_programs(1))

    def start(slot):
        layer = jnp.minimum(map_ref[slot, 0], layers - 1)
        prepare(slot, layer, (idx_ref, val_ref, ids_ref, val_scr, *split_scr), pairs, zs, features)

    def build(slot, part):
        build_span(part, span, acts_ref.at[slot], lows[slot], rows_scr, *split_scr)

    def multiply(slot):
        dhi, dlo = split(dec_ref[0])
        prod = jnp.dot(acts_ref[slot], dhi, preferred_element_type=f32)
        prod += jnp.dot(lows[slot][...], dhi, preferred_element_type=f32)
        prod += jnp.dot(acts_ref[slot], dlo, preferred_element_type=f32)
        keep_ref[0] = prod[:tokens // 2]
        send_ref[0] = prod[tokens // 2:]

    @pl.when((j == 0) & (n == 0))
    def _():
        start(0)

        def part(b, _):
            build(0, b)
            return 0

        lax.fori_loop(0, steps, part, 0)

    for slot in range(slots):
        if slot + 1 < slots:
            @pl.when((j == slot) & (n == 0))
            def _():
                start(slot + 1)

        @pl.when(j == slot)
        def _():
            if slot + 1 < slots:
                for q in range(share):
                    build(slot + 1, jnp.minimum(n * share + q, steps - 1))
            multiply(slot)


def recon_call(pair_map, indices, values, decoder, pairs, zs, tile=RECON_TILE, span=64):
    slots, features, width = decoder.shape
    layers, tokens, active = indices.shape
    tile = min(tile, width)
    blocks = features // LANES
    half = pl.BlockSpec((1, tokens // 2, tile), lambda j, n, m: (j, 0, n))

    def kernel(*refs):
        recon_kernel(slots, layers, pairs, zs, span, *refs)

    def whole(*shape):
        return pl.BlockSpec(shape, lambda j, n, m: (0, 0, 0))

    return pl.pallas_call(
        kernel,
        out_shape=(
            jax.ShapeDtypeStruct((slots, tokens // 2, width), f32),
            jax.ShapeDtypeStruct((slots, tokens // 2, width), f32),
            jax.ShapeDtypeStruct((slots, tokens, features), bf16),
            jax.ShapeDtypeStruct((slots, tokens, active), i32),
        ),
        grid_spec=pltpu.PrefetchScalarGridSpec(
            num_scalar_prefetch=1,
            grid=(slots, width // tile),
            in_specs=[
                whole(layers, tokens, active),
                whole(layers, tokens, active),
                pl.BlockSpec((1, features, tile), lambda j, n, m: (j, 0, n)),
            ],
            out_specs=[half, half, whole(slots, tokens, features), whole(slots, tokens, active)],
            scratch_shapes=[pltpu.VMEM((tokens, features), bf16)] * slots
            + [
                pltpu.VMEM((span * (2 * blocks + 1) + 8, LANES), f32),
                pltpu.VMEM((tokens, active), f32),
                pltpu.VMEM((tokens, active), i32),
                pltpu.VMEM((tokens, active), i32),
                pltpu.VMEM((tokens, active), f32),
                pltpu.VMEM((tokens, active), f32),
            ],
        ),
        compiler_params=params(30),
        cost_estimate=cost(6 * slots * tokens * features * width, 4 * slots * features * width),
        name="recon",
    )(pair_map, indices, values, decoder)


def gather_errors(pieces, err_scr):
    for j in range(err_scr.shape[0]):
        at = 0
        for piece in pieces:
            rows = piece.shape[1]
            err_scr[j, at:at + rows] = piece[j]
            at += rows


def acts_grad(acts_ref, err):
    return lax.dot_general(acts_ref[0], err, TN, preferred_element_type=f32)


def back_kernel(count, slot_steps, ids_ref, acts_ref, dec_ref, *refs):
    pieces, (keep_ref, send_ref, grad_ref, total_scr, err_scr) = refs[:count], refs[count:]
    i = pl.program_id(0)
    j, n = i // slot_steps, lax.rem(i, slot_steps)
    depth, grad_depth = dec_ref.shape[1], grad_ref.shape[1]

    @pl.when(i == 0)
    def _():
        gather_errors(pieces, err_scr)

    @pl.when(n == 0)
    def _():
        total_scr[...] = jnp.zeros_like(total_scr)

    back = lax.dot_general(err_scr[j], dec_ref[0].astype(bf16), NT, preferred_element_type=f32)
    grad_ref[0] = acts_grad(acts_ref, err_scr[i * grad_depth // (slot_steps * depth)])
    ids = ids_ref[0] - n * depth
    block = ids >> 7
    lane = ids & 127
    total = total_scr[...]
    for c in range(depth // LANES):
        picked = jnp.take_along_axis(back[:, c * LANES:(c + 1) * LANES], lane, axis=1)
        total = jnp.where(block == c, picked, total)
    total_scr[...] = total

    @pl.when(n == slot_steps - 1)
    def _():
        half = total.shape[0] // 2
        keep_ref[0] = total[:half]
        send_ref[0] = total[half:]


def back_call(ids, acts, pieces, decoder, depth=BACK_DEPTH):
    slots, features, width = decoder.shape
    _, tokens, active = ids.shape
    depth = min(depth, features)
    grad_depth = depth // 2
    slot_steps = features // depth
    slot_parts = features // grad_depth
    count = len(pieces)

    def kernel(*refs):
        back_kernel(count, slot_steps, *refs)

    half = pl.BlockSpec((1, tokens // 2, active), lambda i: (i // slot_steps, 0, 0))
    return pl.pallas_call(
        kernel,
        out_shape=[jax.ShapeDtypeStruct((slots, tokens // 2, active), f32)] * 2
        + [jax.ShapeDtypeStruct((slots, features, width), f32)],
        grid=(slots * slot_steps,),
        in_specs=[
            pl.BlockSpec((1, tokens, active), lambda i: (i // slot_steps, 0, 0)),
            pl.BlockSpec((1, tokens, grad_depth), lambda i: (i // slot_parts, 0, i % slot_parts)),
            pl.BlockSpec((1, depth, width), lambda i: (i // slot_steps, i % slot_steps, 0)),
        ]
        + [pl.BlockSpec(x.shape, lambda i: (0, 0, 0)) for x in pieces],
        out_specs=[half, half, pl.BlockSpec((1, grad_depth, width), lambda i: (i // slot_parts, i % slot_parts, 0))],
        scratch_shapes=[pltpu.VMEM((tokens, active), f32), pltpu.VMEM((slots, tokens, width), bf16)],
        compiler_params=params(46),
        cost_estimate=cost(3 * slots * tokens * features * width, 6 * slots * features * width),
        name="back",
    )(ids, acts, decoder, *pieces)


def grad_kernel(count, acts_ref, *refs):
    pieces, (grad_ref, err_scr) = refs[:count], refs[-2:]

    @pl.when(pl.program_id(0) == 0)
    def _():
        gather_errors(pieces, err_scr)

    grad_ref[0] = acts_grad(acts_ref, err_scr[0])


def grad_call(acts, pieces, quarter, earlier, depth=512):
    slots, tokens, features = acts.shape
    width = pieces[0].shape[2]
    span = slots * features // 4
    slot, first = quarter * span // features, quarter * span % features
    depth = min(depth, span)
    count = len(pieces)

    def kernel(*refs):
        grad_kernel(count, *refs)

    return pl.pallas_call(
        kernel,
        out_shape=jax.ShapeDtypeStruct((slots, features, width), f32),
        grid=(span // depth,),
        in_specs=[pl.BlockSpec((1, tokens, depth), lambda i: (slot, 0, first // depth + i))]
        + [pl.BlockSpec((1, x.shape[1], width), lambda i: (slot, 0, 0)) for x in pieces]
        + [pl.BlockSpec(memory_space=pl.ANY)],
        out_specs=pl.BlockSpec((1, depth, width), lambda i: (slot, first // depth + i, 0)),
        scratch_shapes=[pltpu.VMEM((1, tokens, width), bf16)],
        input_output_aliases={count + 1: 0},
        compiler_params=params(56),
        cost_estimate=cost(2 * span * tokens * width, 4 * span * width),
        name="grad",
    )(acts, *pieces, earlier)


def layer_sums(tables, blocks, layers):
    shape = blocks[0].shape[1:]

    def kernel(table_ref, *refs):
        out_ref = refs[-1]
        out_ref[...] = jnp.zeros_like(out_ref)
        for m, ref in enumerate(refs[:-1]):
            for j in range(ref.shape[0]):
                goal = table_ref[m, j]

                @pl.when(goal < layers)
                def _():
                    out_ref[goal] = out_ref[goal] + ref[j]

    return pl.pallas_call(
        kernel,
        out_shape=jax.ShapeDtypeStruct((layers,) + shape, f32),
        in_specs=[pl.BlockSpec(memory_space=pltpu.SMEM)] + [pl.BlockSpec(memory_space=pltpu.VMEM)] * len(blocks),
        out_specs=pl.BlockSpec(memory_space=pltpu.VMEM),
        compiler_params=params(8),
        name="layer_sums",
    )(tables, *blocks)


def choose_layers(tables, errors, slots):
    layers, rows, width = errors[0].shape
    if rows % 8:
        column = jnp.concatenate(errors, axis=1)
        out = []
        for table in tables:
            picked = [
                sum(jnp.where(table[j] == layer, column[layer], jnp.zeros((), bf16)) for layer in range(layers))
                for j in range(slots)
            ]
            out.append(jnp.stack(picked))
        return out
    count = tables.shape[0]
    total = len(errors) * rows

    def kernel(table_ref, *refs):
        for m, out_ref in enumerate(refs[len(errors):]):
            for j in range(slots):
                goal = table_ref[m, j]
                at = jnp.minimum(goal, layers - 1)
                live = jnp.where(goal < layers, 1.0, 0.0)
                wide = jnp.concatenate([ref[at].astype(f32) for ref in refs[:len(errors)]], axis=0)
                out_ref[j] = (wide * live).astype(bf16)

    return pl.pallas_call(
        kernel,
        out_shape=[jax.ShapeDtypeStruct((slots, total, width), bf16)] * count,
        in_specs=[pl.BlockSpec(memory_space=pltpu.SMEM)] + [pl.BlockSpec(memory_space=pltpu.VMEM)] * len(errors),
        out_specs=[pl.BlockSpec(memory_space=pltpu.VMEM)] * count,
        compiler_params=params(12),
        name="choose_layers",
    )(tables, *errors)


def swap_cores(x):
    return lax.ppermute(x, "feat", [(i, i ^ 1) for i in range(lax.axis_size("feat"))])


def swap_z(x, m):
    return lax.ppermute(x, "feat", [(i, i ^ (2 * m)) for i in range(lax.axis_size("feat"))])


def swap_pair(x, m):
    return lax.ppermute(x, "pair", [(i, i ^ m) for i in range(lax.axis_size("pair"))])


def pack(x):
    return (x * WIRE_SCALE).astype(jnp.float16)


def unpack(x):
    return x.astype(f32) * (1.0 / WIRE_SCALE)


def weigh(chosen, blocks):
    total = 0.0
    for m, block in enumerate(blocks):
        for j in range(block.shape[0]):
            total = total + chosen[m, j][:, None, None] * block[j][None]
    return total


def sum_full(keep, send, pair_map, layers):
    pairs, zs = lax.axis_size("pair"), lax.axis_size("feat") // 2
    run = keep.shape[1] // pairs
    rows = run // zs
    got = swap_cores(send)
    pair_map, _ = lax.optimization_barrier((pair_map, keep))
    maps = [pair_map] + [swap_pair(pair_map, m) for m in range(1, pairs)]
    halves = [keep[:, m * run:(m + 1) * run] + got[:, m * run:(m + 1) * run] for m in range(pairs)]
    packed = [pack(x) for x in halves[1:]]
    arrived = [None] + [swap_pair(packed[m - 1], m) for m in range(1, pairs)]
    maps, _ = lax.optimization_barrier((jnp.stack(maps), packed))
    sources, goals = maps[:, :, 0], maps[:, :, 1]
    chosen = (goals[:, :, None] == jnp.arange(layers, dtype=i32)).astype(f32)
    chosen, sources, goals = lax.optimization_barrier((chosen, sources, goals))
    parts = []
    for k in range(zs):
        cut = slice(k * rows, (k + 1) * rows)
        blocks = [halves[0][:, cut]] + [unpack(x[:, cut]) for x in arrived[1:]]
        parts.append(weigh(chosen, blocks))
    sent = [pack(x) for x in parts[1:]]
    full = parts[0]
    for m in range(1, zs):
        full = full + unpack(swap_z(sent[m - 1], m))
    return full, sources, goals


def spread_errors(error, goals, slots):
    pairs, zs = lax.axis_size("pair"), lax.axis_size("feat") // 2
    errors = [error] + [swap_z(error, m) for m in range(1, zs)]
    chosen = choose_layers(goals, errors, slots)
    own = [chosen[0]] + [swap_pair(chosen[m], m) for m in range(1, pairs)]
    return own + [swap_cores(x) for x in own]


def finish(keep, send, sources, layers, acts, pieces, dec_grad):
    pairs, zs = lax.axis_size("pair"), lax.axis_size("feat") // 2
    slots, half_rows, width = keep.shape
    rows = half_rows // (pairs * zs)
    half = (keep + swap_cores(send)).reshape(slots, pairs, zs, rows, width)
    arrived = [half[:, :, 0]] + [swap_z(half[:, :, m], m) for m in range(1, zs)]
    dec_grad = grad_call(acts, pieces, 2, dec_grad)
    dec_grad, *arrived = lax.optimization_barrier((dec_grad, *arrived))
    column = sum(arrived)
    arrived = [column[:, 0]] + [swap_pair(column[:, m], m) for m in range(1, pairs)]
    dec_grad = grad_call(acts, pieces, 3, dec_grad)
    dec_grad, *arrived = lax.optimization_barrier((dec_grad, *arrived))
    return dec_grad, layer_sums(sources, arrived, layers)


def body(decoder, pair_map, indices, values, target):
    slots = decoder.shape[0]
    layers = indices.shape[0]
    pairs, zs = lax.axis_size("pair"), lax.axis_size("feat") // 2
    keep, send, acts, ids = recon_call(pair_map, indices, values, decoder, pairs, zs)
    full, sources, goals = sum_full(keep, send, pair_map, layers)
    recon = full.astype(bf16)
    error = (full - target).astype(bf16)
    pieces = spread_errors(error, goals, slots)
    keep, send, dec_grad = back_call(ids, acts, pieces, decoder)
    dec_grad, feat_grad = finish(keep, send, sources, layers, acts, pieces, dec_grad)
    return recon, dec_grad, feat_grad


def solution(mesh):
    in_specs = (P("pair", "feat", None), P("pair", None), P(), P(), P(None, ("pair", "feat"), None))
    out_specs = (
        P(None, ("pair", "feat"), None),
        P("pair", "feat", None),
        P(None, ("pair", "feat"), None),
    )
    return jax.shard_map(body, mesh=mesh, in_specs=in_specs, out_specs=out_specs, check_vma=False)
```

```python
import jax
import jax.numpy as jnp
from jax import lax
from jax.experimental import pallas as pl
from jax.experimental.pallas import tpu as pltpu
from jax.sharding import PartitionSpec as P

f32 = jnp.float32
bf16 = jnp.bfloat16
i32 = jnp.int32
LANES = 128
WIRE_SCALE = 128.0
BACK_DEPTH = 1024
RECON_TILE = 512
NT = (((1,), (1,)), ((), ()))
TN = (((0,), (0,)), ((), ()))


def split(x):
    hi = x.astype(bf16)
    return hi, (x - hi.astype(f32)).astype(bf16)


def cost(flops, nbytes):
    return pl.CostEstimate(flops=int(flops), bytes_accessed=int(nbytes), transcendentals=0)


def params(mib):
    return pltpu.CompilerParams(vmem_limit_bytes=mib << 20)


def prepare(slot, layer, refs, pairs, zs, features):
    idx_ref, val_ref, ids_ref, val_scr, hi_scr, lo_scr, vhi_scr, vlo_scr = refs
    tokens = idx_ref.shape[1]
    rows = tokens // (pairs * zs * 2)
    p, feat = lax.axis_index("pair"), lax.axis_index("feat")
    first = feat * features

    def run(at, _):
        zr = at & (zs - 1)
        pr = (at // zs) & (pairs - 1)
        cr = at // (zs * pairs)
        block = (p ^ pr) * (zs * 2) + (feat ^ (zr * 2 + cr))
        ids_ref[slot, pl.ds(at * rows, rows), :] = idx_ref[layer, pl.ds(block * rows, rows), :] - first
        val_scr[pl.ds(at * rows, rows), :] = val_ref[layer, pl.ds(block * rows, rows), :]
        return 0

    lax.fori_loop(0, tokens // rows, run, 0)
    ids = ids_ref[slot]
    vhi, vlo = split(val_scr[...])
    hi_scr[...] = ids >> 7
    lo_scr[...] = ids & 127
    vhi_scr[...] = vhi.astype(f32)
    vlo_scr[...] = vlo.astype(f32)


def build_span(part, span, high_ref, low_ref, rows_scr, hi_scr, lo_scr, vhi_scr, vlo_scr):
    active = hi_scr.shape[1]
    blocks = high_ref.shape[-1] // LANES
    pitch = 2 * blocks + 1
    iota_block = lax.broadcasted_iota(i32, (blocks, active), 0)
    iota_lane = lax.broadcasted_iota(i32, (LANES, active), 0)
    empty = jnp.zeros((2 * blocks, active), bf16)
    base = pl.multiple_of(part * span, span)

    def factors(at):
        def row(ref, count):
            return jnp.broadcast_to(ref[pl.ds(at, 1), :], (count, active))

        hit = row(hi_scr, blocks) == iota_block
        high = jnp.where(hit, row(vhi_scr, blocks), 0.0)
        low = jnp.where(hit, row(vlo_scr, blocks), 0.0)
        weights = jnp.concatenate([high, low], axis=0).astype(bf16)
        onehot = jnp.where(row(lo_scr, LANES) == iota_lane, 1.0, 0.0).astype(bf16)
        return weights, onehot

    for i in range(0, span, 2):
        w0, o0 = factors(base + i)
        w1, o1 = factors(base + i + 1)
        weights = jnp.concatenate(
            [jnp.concatenate([w0, empty], axis=1), jnp.concatenate([empty, w1], axis=1)], axis=0
        )
        onehot = jnp.concatenate([o0, o1], axis=1)
        got = lax.dot_general(weights, onehot, NT, preferred_element_type=f32)
        rows_scr[i * pitch:i * pitch + 2 * blocks, :] = got[:2 * blocks]
        rows_scr[(i + 1) * pitch:(i + 1) * pitch + 2 * blocks, :] = got[2 * blocks:]
    for h in range(blocks):
        lanes = slice(h * LANES, (h + 1) * LANES)
        high = rows_scr[pl.ds(h, span, stride=pitch), :]
        low = rows_scr[pl.ds(blocks + h, span, stride=pitch), :]
        high_ref[pl.ds(base, span), lanes] = high.astype(bf16)
        low_ref[pl.ds(base, span), lanes] = low.astype(bf16)


def recon_kernel(slots, layers, pairs, zs, span, map_ref, idx_ref, val_ref, dec_ref, keep_ref, send_ref, acts_ref, ids_ref, *scr):
    lows, (rows_scr, val_scr, *split_scr) = scr[:slots], scr[slots:]
    _, tokens, features = acts_ref.shape
    j, n = pl.program_id(0), pl.program_id(1)
    steps = tokens // span
    share = -(-steps // pl.num_programs(1))

    def start(slot):
        layer = jnp.minimum(map_ref[slot, 0], layers - 1)
        prepare(slot, layer, (idx_ref, val_ref, ids_ref, val_scr, *split_scr), pairs, zs, features)

    def build(slot, part):
        build_span(part, span, acts_ref.at[slot], lows[slot], rows_scr, *split_scr)

    def multiply(slot):
        dhi, dlo = split(dec_ref[0])
        prod = jnp.dot(acts_ref[slot], dhi, preferred_element_type=f32)
        prod += jnp.dot(lows[slot][...], dhi, preferred_element_type=f32)
        prod += jnp.dot(acts_ref[slot], dlo, preferred_element_type=f32)
        keep_ref[0] = prod[:tokens // 2]
        send_ref[0] = prod[tokens // 2:]

    @pl.when((j == 0) & (n == 0))
    def _():
        start(0)

        def part(b, _):
            build(0, b)
            return 0

        lax.fori_loop(0, steps, part, 0)

    for slot in range(slots):
        if slot + 1 < slots:
            @pl.when((j == slot) & (n == 0))
            def _():
                start(slot + 1)

        @pl.when(j == slot)
        def _():
            if slot + 1 < slots:
                for q in range(share):
                    build(slot + 1, jnp.minimum(n * share + q, steps - 1))
            multiply(slot)


def recon_call(pair_map, indices, values, decoder, pairs, zs, tile=RECON_TILE, span=64):
    slots, features, width = decoder.shape
    layers, tokens, active = indices.shape
    tile = min(tile, width)
    blocks = features // LANES
    half = pl.BlockSpec((1, tokens // 2, tile), lambda j, n, m: (j, 0, n))

    def kernel(*refs):
        recon_kernel(slots, layers, pairs, zs, span, *refs)

    def whole(*shape):
        return pl.BlockSpec(shape, lambda j, n, m: (0, 0, 0))

    return pl.pallas_call(
        kernel,
        out_shape=(
            jax.ShapeDtypeStruct((slots, tokens // 2, width), f32),
            jax.ShapeDtypeStruct((slots, tokens // 2, width), f32),
            jax.ShapeDtypeStruct((slots, tokens, features), bf16),
            jax.ShapeDtypeStruct((slots, tokens, active), i32),
        ),
        grid_spec=pltpu.PrefetchScalarGridSpec(
            num_scalar_prefetch=1,
            grid=(slots, width // tile),
            in_specs=[
                whole(layers, tokens, active),
                whole(layers, tokens, active),
                pl.BlockSpec((1, features, tile), lambda j, n, m: (j, 0, n)),
            ],
            out_specs=[half, half, whole(slots, tokens, features), whole(slots, tokens, active)],
            scratch_shapes=[pltpu.VMEM((tokens, features), bf16)] * slots
            + [
                pltpu.VMEM(((span + 1) * (2 * blocks + 1) + 8, LANES), f32),
                pltpu.VMEM((tokens, active), f32),
                pltpu.VMEM((tokens, active), i32),
                pltpu.VMEM((tokens, active), i32),
                pltpu.VMEM((tokens, active), f32),
                pltpu.VMEM((tokens, active), f32),
            ],
        ),
        compiler_params=params(30),
        cost_estimate=cost(6 * slots * tokens * features * width, 4 * slots * features * width),
        name="recon",
    )(pair_map, indices, values, decoder)


def gather_errors(pieces, err_scr):
    for j in range(err_scr.shape[0]):
        at = 0
        for piece in pieces:
            rows = piece.shape[1]
            err_scr[j, at:at + rows] = piece[j]
            at += rows


def acts_grad(acts_ref, err):
    return lax.dot_general(acts_ref[0], err, TN, preferred_element_type=f32)


def back_kernel(count, slot_steps, ids_ref, acts_ref, dec_ref, *refs):
    pieces, (keep_ref, send_ref, grad_ref, total_scr, err_scr) = refs[:count], refs[count:]
    i = pl.program_id(0)
    j, n = i // slot_steps, lax.rem(i, slot_steps)
    depth, grad_depth = dec_ref.shape[1], grad_ref.shape[1]

    @pl.when(i == 0)
    def _():
        gather_errors(pieces, err_scr)

    @pl.when(n == 0)
    def _():
        total_scr[...] = jnp.zeros_like(total_scr)

    back = lax.dot_general(err_scr[j], dec_ref[0].astype(bf16), NT, preferred_element_type=f32)
    grad_ref[0] = acts_grad(acts_ref, err_scr[i * grad_depth // (slot_steps * depth)])
    ids = ids_ref[0] - n * depth
    block = ids >> 7
    lane = ids & 127
    total = total_scr[...]
    for c in range(depth // LANES):
        picked = jnp.take_along_axis(back[:, c * LANES:(c + 1) * LANES], lane, axis=1)
        total = jnp.where(block == c, picked, total)
    total_scr[...] = total

    @pl.when(n == slot_steps - 1)
    def _():
        half = total.shape[0] // 2
        keep_ref[0] = total[:half]
        send_ref[0] = total[half:]


def back_call(ids, acts, pieces, decoder, depth=BACK_DEPTH):
    slots, features, width = decoder.shape
    _, tokens, active = ids.shape
    depth = min(depth, features)
    grad_depth = depth // 2
    slot_steps = features // depth
    slot_parts = features // grad_depth
    count = len(pieces)

    def kernel(*refs):
        back_kernel(count, slot_steps, *refs)

    half = pl.BlockSpec((1, tokens // 2, active), lambda i: (i // slot_steps, 0, 0))
    return pl.pallas_call(
        kernel,
        out_shape=[jax.ShapeDtypeStruct((slots, tokens // 2, active), f32)] * 2
        + [jax.ShapeDtypeStruct((slots, features, width), f32)],
        grid=(slots * slot_steps,),
        in_specs=[
            pl.BlockSpec((1, tokens, active), lambda i: (i // slot_steps, 0, 0)),
            pl.BlockSpec((1, tokens, grad_depth), lambda i: (i // slot_parts, 0, i % slot_parts)),
            pl.BlockSpec((1, depth, width), lambda i: (i // slot_steps, i % slot_steps, 0)),
        ]
        + [pl.BlockSpec(x.shape, lambda i: (0, 0, 0)) for x in pieces],
        out_specs=[half, half, pl.BlockSpec((1, grad_depth, width), lambda i: (i // slot_parts, i % slot_parts, 0))],
        scratch_shapes=[pltpu.VMEM((tokens, active), f32), pltpu.VMEM((slots, tokens, width), bf16)],
        compiler_params=params(46),
        cost_estimate=cost(3 * slots * tokens * features * width, 6 * slots * features * width),
        name="back",
    )(ids, acts, decoder, *pieces)


def grad_kernel(count, acts_ref, *refs):
    pieces, (grad_ref, err_scr) = refs[:count], refs[-2:]

    @pl.when(pl.program_id(0) == 0)
    def _():
        gather_errors(pieces, err_scr)

    grad_ref[0] = acts_grad(acts_ref, err_scr[0])


def grad_call(acts, pieces, quarter, earlier, depth=512):
    slots, tokens, features = acts.shape
    width = pieces[0].shape[2]
    span = slots * features // 4
    slot, first = quarter * span // features, quarter * span % features
    depth = min(depth, span)
    count = len(pieces)

    def kernel(*refs):
        grad_kernel(count, *refs)

    return pl.pallas_call(
        kernel,
        out_shape=jax.ShapeDtypeStruct((slots, features, width), f32),
        grid=(span // depth,),
        in_specs=[pl.BlockSpec((1, tokens, depth), lambda i: (slot, 0, first // depth + i))]
        + [pl.BlockSpec((1, x.shape[1], width), lambda i: (slot, 0, 0)) for x in pieces]
        + [pl.BlockSpec(memory_space=pl.ANY)],
        out_specs=pl.BlockSpec((1, depth, width), lambda i: (slot, first // depth + i, 0)),
        scratch_shapes=[pltpu.VMEM((1, tokens, width), bf16)],
        input_output_aliases={count + 1: 0},
        compiler_params=params(56),
        cost_estimate=cost(2 * span * tokens * width, 4 * span * width),
        name="grad",
    )(acts, *pieces, earlier)


def layer_sums(tables, blocks, layers):
    shape = blocks[0].shape[1:]

    def kernel(table_ref, *refs):
        out_ref = refs[-1]
        out_ref[...] = jnp.zeros_like(out_ref)
        for m, ref in enumerate(refs[:-1]):
            for j in range(ref.shape[0]):
                goal = table_ref[m, j]

                @pl.when(goal < layers)
                def _():
                    out_ref[goal] = out_ref[goal] + ref[j]

    return pl.pallas_call(
        kernel,
        out_shape=jax.ShapeDtypeStruct((layers,) + shape, f32),
        in_specs=[pl.BlockSpec(memory_space=pltpu.SMEM)] + [pl.BlockSpec(memory_space=pltpu.VMEM)] * len(blocks),
        out_specs=pl.BlockSpec(memory_space=pltpu.VMEM),
        compiler_params=params(8),
        name="layer_sums",
    )(tables, *blocks)


def choose_layers(tables, errors, slots):
    layers, rows, width = errors[0].shape
    if rows % 8:
        column = jnp.concatenate(errors, axis=1)
        out = []
        for table in tables:
            picked = [
                sum(jnp.where(table[j] == layer, column[layer], jnp.zeros((), bf16)) for layer in range(layers))
                for j in range(slots)
            ]
            out.append(jnp.stack(picked))
        return out
    count = tables.shape[0]
    total = len(errors) * rows

    def kernel(table_ref, *refs):
        for m, out_ref in enumerate(refs[len(errors):]):
            for j in range(slots):
                goal = table_ref[m, j]
                at = jnp.minimum(goal, layers - 1)
                live = jnp.where(goal < layers, 1.0, 0.0)
                wide = jnp.concatenate([ref[at].astype(f32) for ref in refs[:len(errors)]], axis=0)
                out_ref[j] = (wide * live).astype(bf16)

    return pl.pallas_call(
        kernel,
        out_shape=[jax.ShapeDtypeStruct((slots, total, width), bf16)] * count,
        in_specs=[pl.BlockSpec(memory_space=pltpu.SMEM)] + [pl.BlockSpec(memory_space=pltpu.VMEM)] * len(errors),
        out_specs=[pl.BlockSpec(memory_space=pltpu.VMEM)] * count,
        compiler_params=params(12),
        name="choose_layers",
    )(tables, *errors)


def swap_cores(x):
    return lax.ppermute(x, "feat", [(i, i ^ 1) for i in range(lax.axis_size("feat"))])


def swap_z(x, m):
    return lax.ppermute(x, "feat", [(i, i ^ (2 * m)) for i in range(lax.axis_size("feat"))])


def swap_pair(x, m):
    return lax.ppermute(x, "pair", [(i, i ^ m) for i in range(lax.axis_size("pair"))])


def pack(x):
    return (x * WIRE_SCALE).astype(jnp.float16)


def unpack(x):
    return x.astype(f32) * (1.0 / WIRE_SCALE)


def weigh(chosen, blocks):
    total = 0.0
    for m, block in enumerate(blocks):
        for j in range(block.shape[0]):
            total = total + chosen[m, j][:, None, None] * block[j][None]
    return total


def sum_full(keep, send, pair_map, layers):
    pairs, zs = lax.axis_size("pair"), lax.axis_size("feat") // 2
    run = keep.shape[1] // pairs
    rows = run // zs
    got = swap_cores(send)
    pair_map, _ = lax.optimization_barrier((pair_map, keep))
    maps = [pair_map] + [swap_pair(pair_map, m) for m in range(1, pairs)]
    halves = [keep[:, m * run:(m + 1) * run] + got[:, m * run:(m + 1) * run] for m in range(pairs)]
    packed = [pack(x) for x in halves[1:]]
    arrived = [None] + [swap_pair(packed[m - 1], m) for m in range(1, pairs)]
    maps, _ = lax.optimization_barrier((jnp.stack(maps), packed))
    sources, goals = maps[:, :, 0], maps[:, :, 1]
    chosen = (goals[:, :, None] == jnp.arange(layers, dtype=i32)).astype(f32)
    chosen, sources, goals = lax.optimization_barrier((chosen, sources, goals))
    parts = []
    for k in range(zs):
        cut = slice(k * rows, (k + 1) * rows)
        blocks = [halves[0][:, cut]] + [unpack(x[:, cut]) for x in arrived[1:]]
        parts.append(weigh(chosen, blocks))
    sent = [pack(x) for x in parts[1:]]
    full = parts[0]
    for m in range(1, zs):
        full = full + unpack(swap_z(sent[m - 1], m))
    return full, sources, goals


def spread_errors(error, goals, slots):
    pairs, zs = lax.axis_size("pair"), lax.axis_size("feat") // 2
    errors = [error] + [swap_z(error, m) for m in range(1, zs)]
    chosen = choose_layers(goals, errors, slots)
    own = [chosen[0]] + [swap_pair(chosen[m], m) for m in range(1, pairs)]
    return own + [swap_cores(x) for x in own]


def finish(keep, send, sources, layers, acts, pieces, dec_grad):
    pairs, zs = lax.axis_size("pair"), lax.axis_size("feat") // 2
    slots, half_rows, width = keep.shape
    rows = half_rows // (pairs * zs)
    half = (keep + swap_cores(send)).reshape(slots, pairs, zs, rows, width)
    arrived = [half[:, :, 0]] + [swap_z(half[:, :, m], m) for m in range(1, zs)]
    dec_grad = grad_call(acts, pieces, 2, dec_grad)
    dec_grad, *arrived = lax.optimization_barrier((dec_grad, *arrived))
    column = sum(arrived)
    arrived = [column[:, 0]] + [swap_pair(column[:, m], m) for m in range(1, pairs)]
    dec_grad = grad_call(acts, pieces, 3, dec_grad)
    dec_grad, *arrived = lax.optimization_barrier((dec_grad, *arrived))
    return dec_grad, layer_sums(sources, arrived, layers)


def body(decoder, pair_map, indices, values, target):
    slots = decoder.shape[0]
    layers = indices.shape[0]
    pairs, zs = lax.axis_size("pair"), lax.axis_size("feat") // 2
    keep, send, acts, ids = recon_call(pair_map, indices, values, decoder, pairs, zs)
    full, sources, goals = sum_full(keep, send, pair_map, layers)
    recon = full.astype(bf16)
    error = (full - target).astype(bf16)
    pieces = spread_errors(error, goals, slots)
    keep, send, dec_grad = back_call(ids, acts, pieces, decoder)
    dec_grad, feat_grad = finish(keep, send, sources, layers, acts, pieces, dec_grad)
    return recon, dec_grad, feat_grad


def solution(mesh):
    in_specs = (P("pair", "feat", None), P("pair", None), P(), P(), P(None, ("pair", "feat"), None))
    out_specs = (
        P(None, ("pair", "feat"), None),
        P("pair", "feat", None),
        P(None, ("pair", "feat"), None),
    )
    return jax.shard_map(body, mesh=mesh, in_specs=in_specs, out_specs=out_specs, check_vma=False)
```
